512 devices in a mesh: row: 32 (over x, z), col: 16 (over y, core).
Axes of the slice: x: 4, y: 8, z: 8, core: 2. Of those that a mesh axis runs over, the one named last changes fastest.
Arguments:
- prior_solved: float32 [49152, 512], P('row', 'col'), may hold values from -6 to 6
- block_one: float32 [2048, 49152], P('col', 'row'), may hold values from -0.02734375 to 0.02734375
- block_two: float32 [2048, 49152], P('col', 'row'), may hold values from -0.02734375 to 0.02734375
- cross_block: float32 [2048, 2048], P('col', 'row'), may hold values from -0.125 to 0.125
- inverse_one: float32 [2048, 2048], P('row', 'col'), may hold values from -1 to 2, as said below
- inverse_two: float32 [2048, 2048], P('row', 'col'), may hold values from -1 to 2, as said below
- rhs_one: float32 [2048, 512], P('col', 'row'), may hold values from -6 to 6
- rhs_two: float32 [2048, 512], P('col', 'row'), may hold values from -6 to 6
Outputs:
- solved_one: float32 [2048, 512], P('col', 'row')
- solved_two: float32 [2048, 512], P('col', 'row')
The draws below stay inside these ranges and needn't reach their ends.
Inputs may be any that keep to these rules, and one draw needn't show every extreme that they name: `inverse_one`: lower triangular: zero above the diagonal. `inverse_two`: lower triangular: zero above the diagonal.
All inputs are finite; a program needn't handle non-finite values.
Results may differ from the reference program's by a relative error of at most 0.00011.
Values sent between devices are 32-bit elements; how exact they have to be, the bound alone decides.
A program may use at most 64 MiB of HBM per device.

```python
import jax
import jax.numpy as jnp
from jax import lax

H = 2048
W = 512
P_SIZE = 49152


def lower_factor(off_part, diag_part):
    row_ids = lax.broadcasted_iota(jnp.int32, (H, H), 0)
    col_ids = lax.broadcasted_iota(jnp.int32, (H, H), 1)
    scaled = off_part * (0.8 * H ** (-0.5))
    lower = jnp.where(row_ids > col_ids, scaled, jnp.zeros_like(scaled))
    return lower + jnp.where(row_ids == col_ids, diag_part[:, None] * jnp.ones((1, H), jnp.float32), jnp.zeros_like(scaled))


def draw_inverse_one(key, part):
    key = jax.random.fold_in(key, 11)
    off_key, diag_key = jax.random.split(key)
    off_part = jax.random.truncated_normal(off_key, -3.0, 3.0, (H, H), jnp.float32)
    diag_part = jax.random.uniform(diag_key, (H,), jnp.float32, 0.7, 1.4)
    return lower_factor(off_part, diag_part)


def draw_inverse_two(key, part):
    key = jax.random.fold_in(key, 12)
    off_key, diag_key = jax.random.split(key)
    off_part = jax.random.truncated_normal(off_key, -3.0, 3.0, (H, H), jnp.float32)
    diag_part = jax.random.uniform(diag_key, (H,), jnp.float32, 0.7, 1.4)
    return lower_factor(off_part, diag_part)


def block_levels(own_key, dims, pieces, low, largest):
    def one(dim, blocks):
        draws = jax.random.uniform(jax.random.fold_in(jax.random.fold_in(own_key, 6), dim), (blocks,), jnp.float32, low / len(pieces), largest / len(pieces))
        return jnp.repeat(jnp.exp(draws), dims[dim] // blocks).reshape((-1,) + (1,) * (len(dims) - dim - 1))

    gain = one(*pieces[0])
    for cut in pieces[1:]:
        gain = gain * one(*cut)
    return gain


def noise(stream_key, dims, scale, limit, cuts=(), held_as=jnp.bfloat16):
    array = jax.random.normal(stream_key, dims, jnp.float32) * scale
    if len(cuts) > 0:
        array = block_levels(stream_key, dims, cuts, -0.22, 0.18) * array
    return jnp.clip(array, min=-limit, max=limit).astype(held_as)


def setup_inputs(seed: int = 0) -> dict:
    splits = jax.random.split(jax.random.key(seed), 9)
    prior_solved = noise(splits[0], (P_SIZE, W), 1.0, 6.0, ((0, 32), (1, 16)), jnp.float32)
    block_one = noise(splits[1], (H, P_SIZE), P_SIZE ** -0.5, 0.02734375, ((0, 16), (1, 32)), jnp.float32)
    block_two = noise(splits[2], (H, P_SIZE), P_SIZE ** -0.5, 0.02734375, ((0, 16), (1, 32)), jnp.float32)
    cross_block = noise(splits[3], (H, H), H ** -0.5, 0.125, ((0, 16), (1, 32)), jnp.float32)
    inverse_one = draw_inverse_one(jax.random.fold_in(splits[8], 71), 0)
    inverse_two = draw_inverse_two(jax.random.fold_in(splits[8], 71), 0)
    rhs_one = noise(splits[6], (H, W), 1.0, 6.0, ((0, 16), (1, 32)), jnp.float32)
    rhs_two = noise(splits[7], (H, W), 1.0, 6.0, ((0, 16), (1, 32)), jnp.float32)
    return {"prior_solved": prior_solved, "block_one": block_one, "block_two": block_two, "cross_block": cross_block, "inverse_one": inverse_one, "inverse_two": inverse_two, "rhs_one": rhs_one, "rhs_two": rhs_two}


def reference(prior_solved, block_one, block_two, cross_block, inverse_one, inverse_two, rhs_one, rhs_two):
    highest = lax.Precision.HIGHEST
    first_sum = jnp.dot(block_one, prior_solved, precision=highest, preferred_element_type=jnp.float32)
    second_sum = jnp.dot(block_two, prior_solved, precision=highest, preferred_element_type=jnp.float32)
    solved_one = jnp.dot(inverse_one, rhs_one - first_sum, precision=highest, preferred_element_type=jnp.float32)
    coupled = jnp.dot(cross_block, solved_one, precision=highest, preferred_element_type=jnp.float32)
    solved_two = jnp.dot(inverse_two, rhs_two - second_sum - coupled, precision=highest, preferred_element_type=jnp.float32)
    return solved_one, solved_two
```

```python
import functools

import jax
import jax.numpy as jnp
from jax import lax
from jax.experimental import pallas as pl
from jax.experimental.pallas import tpu as pltpu
from jax.sharding import PartitionSpec as P

NX, NZ, NY = 4, 8, 8
NC = 2 * NY
DEPTH = 1536
MESH = pl.DeviceIdType.MESH
F32 = jnp.float32
BF16 = jnp.bfloat16


def split(a):
    high = a.astype(BF16)
    return high, (a - high.astype(F32)).astype(BF16)


def dot3(a, b_high, b_low, contract):
    high, low = split(a)
    rows = a.shape[0]
    dims = (((1,), (contract,)), ((), ()))
    both = lax.dot_general(
        jnp.concatenate([high, low], axis=0), b_high, dims, preferred_element_type=F32
    )
    cross = lax.dot_general(high, b_low, dims, preferred_element_type=F32)
    return both[:rows] + both[rows:] + cross


def kernel(
    prior, block_one, block_two, cross, inv_one, inv_two, rhs_one, rhs_two,
    out_one, out_two,
    slab, blocks, b_high, b_low, mats, m_high, m_low, rhs,
    f_send, z_slots, x_send, x_slots, t_send, t_slots, s_own, s_full, c_send, c_slots,
    u_send, u_slots, s_out,
    load_sem, y_send, y_recv, p_send, p_recv, zr_send, zr_recv,
    f_sem, z_recv, xs_sem, x_recv, stage_send, stage_recv,
):
    row, col = lax.axis_index("row"), lax.axis_index("col")
    x, z = row // NZ, row % NZ
    y, core = col // 2, col % 2
    own_x = col // 4

    def at(xx, zz, cc):
        return (NZ * xx + zz, cc)

    barrier = pltpu.get_barrier_semaphore()

    def greet(device):
        pl.semaphore_signal(barrier, inc=1, device_id=device, device_id_type=MESH)

    for d in range(1, NC):
        greet(at(x, z, (col + d) % NC))
    for d in range(1, NZ):
        greet(at(x, (z + d) % NZ, col))
    for d in range(1, NX):
        greet(at((x + d) % NX, z, col))
    is_own = own_x == x
    for c in range(NC):
        @pl.when(jnp.logical_not(jnp.logical_and(is_own, col == c)))
        def _():
            greet(at(own_x, z, c))

    loads = [
        pltpu.make_async_copy(block_one, blocks.at[0], load_sem.at[0]),
        pltpu.make_async_copy(block_two, blocks.at[1], load_sem.at[1]),
        pltpu.make_async_copy(prior.at[pl.ds(0, 16)], slab.at[0, 0, 0], load_sem.at[2]),
        pltpu.make_async_copy(prior.at[pl.ds(16, 16)], slab.at[0, 0, 1], load_sem.at[3]),
        pltpu.make_async_copy(inv_one, mats.at[z, 0], load_sem.at[4]),
        pltpu.make_async_copy(inv_two, mats.at[z, 1], load_sem.at[5]),
        pltpu.make_async_copy(cross, mats.at[z, 2], load_sem.at[6]),
        pltpu.make_async_copy(rhs_one, rhs.at[0], load_sem.at[7]),
        pltpu.make_async_copy(rhs_two, rhs.at[1], load_sem.at[8]),
    ]
    for i in (2, 3, 4, 5, 6, 0, 1, 7, 8):
        loads[i].start()

    pl.semaphore_wait(
        barrier, (NC - 1) + (NZ - 1) + (NX - 1) + NC - is_own.astype(jnp.int32)
    )

    up, down = at(x, z, (col + 2) % NC), at(x, z, (col + NC - 2) % NC)
    mate = at(x, z, 2 * y + 1 - core)

    def remote(src, dst, send, recv, device):
        return pltpu.make_async_remote_copy(
            src_ref=src, dst_ref=dst, send_sem=send, recv_sem=recv,
            device_id=device, device_id_type=MESH,
        )

    def place(way, j):
        step = j // 2 + 1
        half = j % 2 if way == 0 else 1 - j % 2
        slot = 7 if step == 4 else (step if way == 0 else 3 + step)
        return slot, half

    ring = {}
    for way, device in ((0, up), (1, down)):
        for j in range(7):
            slot, half = place(way, j)
            if j < 2:
                src = prior.at[pl.ds(16 * half, 16)]
            else:
                before, same = place(way, j - 2)
                src = slab.at[0, before, half]
            ring[way, j] = remote(
                src, slab.at[0, slot, half], y_send.at[way, j], y_recv.at[way, j], device
            )
    for j in range(2):
        for way in range(2):
            ring[way, j].start()

    hand = {}
    for half in range(2):
        hand[half, -1] = remote(
            prior.at[pl.ds(16 * half, 16)], slab.at[1, 0, half],
            p_send.at[half, 7], p_recv.at[half, 7], mate,
        )
        hand[half, -1].start()
    for way in range(2):
        for j in range(7):
            slot, half = place(way, j)
            hand[way, j] = remote(
                slab.at[0, slot, half], slab.at[1, slot, half],
                p_send.at[way, j], p_recv.at[way, j], mate,
            )

    z_up, z_down = at(x, (z + 1) % NZ, col), at(x, (z + NZ - 1) % NZ, col)
    z_ring = {}
    for way, device, steps in ((0, z_up, 4), (1, z_down, 3)):
        for step in range(1, steps + 1):
            owner = (z - (step - 1) + NZ) % NZ if way == 0 else (z + step - 1) % NZ
            z_ring[way, step] = remote(
                mats.at[owner], mats.at[owner],
                zr_send.at[way, step - 1], zr_recv.at[way, step - 1], device,
            )

    def z_wait(way, step):
        owner = (z - step + NZ) % NZ if way == 0 else (z + step) % NZ
        pltpu.make_async_copy(
            mats.at[owner], mats.at[owner], zr_recv.at[way, step - 1]
        ).wait()

    for i in (4, 5, 6):
        loads[i].wait()
    for way in range(2):
        z_ring[way, 1].start()

    for b in range(2):
        loads[b].wait()
        for r in range(0, 128, 32):
            high, low = split(blocks[b, r:r + 32, :])
            b_high[128 * b + r:128 * b + r + 32, :] = high
            b_low[128 * b + r:128 * b + r + 32, :] = low
    for i in (2, 3, 7, 8):
        loads[i].wait()

    def product(j, pieces):
        a = jnp.concatenate([slab[b, s, h] for b, s, h, _, _ in pieces], axis=0)
        f = dot3(a, b_high[...], b_low[...], 1)
        for i, (_, _, half, py, pcore) in enumerate(pieces):
            index = 4 * (j + 1) + i
            f_send[index] = f[16 * i:16 * i + 16, :]
            owner_z = 4 * (py % 2) + 2 * pcore + half
            owner_x = py // 2

            @pl.when(owner_z == z)
            def _():
                z_slots[owner_x, 0] = f_send[index]

            @pl.when(owner_z != z)
            def _():
                remote(
                    f_send.at[index], z_slots.at[owner_x, (z - owner_z + NZ) % NZ],
                    f_sem.at[index], z_recv.at[owner_x], at(x, owner_z, col),
                ).start()

    def product_done(j, pieces):
        for i, (_, _, half, py, pcore) in enumerate(pieces):
            index = 4 * (j + 1) + i
            owner_z = 4 * (py % 2) + 2 * pcore + half

            @pl.when(owner_z != z)
            def _():
                pltpu.make_async_copy(
                    f_send.at[index], f_send.at[index], f_sem.at[index]
                ).wait()

    def pieces_of(j):
        if j < 0:
            return [
                (0, 0, 0, y, core), (0, 0, 1, y, core),
                (1, 0, 0, y, 1 - core), (1, 0, 1, y, 1 - core),
            ]
        step = j // 2 + 1
        low_y, high_y = (y + NY - step) % NY, (y + step) % NY
        (s0, h0), (s1, h1) = place(0, j), place(1, j)
        return [
            (0, s0, h0, low_y, core), (0, s1, h1, high_y, core),
            (1, s0, h0, low_y, 1 - core), (1, s1, h1, high_y, 1 - core),
        ]

    odd = jnp.where(y % 2 == z // 4, 0, 1)

    def over_x(q):
        shift = (0 + odd, 2 - 3 * odd, -2 + 5 * odd, 4 - 7 * odd)[q]
        which = ((y + shift + NY) % NY) // 2
        pltpu.make_async_copy(
            z_slots.at[which, pl.ds(1, NZ - 1)], z_slots.at[which, pl.ds(1, NZ - 1)],
            z_recv.at[which],
        ).wait()
        total = z_slots[which, 0]
        for d in range(1, NZ):
            total = total + z_slots[which, d]
        mine = jnp.where(which == x, 1.0, 0.0).astype(F32)
        part = jnp.concatenate([rhs[0], rhs[1]], axis=1) * mine - total
        x_slots[which, 0] = part
        x_send[q] = part
        for d in range(1, NX):
            remote(
                x_send.at[q], x_slots.at[which, NX - d],
                xs_sem.at[q, d - 1], x_recv.at[which], at((x + d) % NX, z, col),
            ).start()

    def over_x_done(q):
        for d in range(1, NX):
            pltpu.make_async_copy(x_send.at[q], x_send.at[q], xs_sem.at[q, d - 1]).wait()

    for half in range(2):
        hand[half, -1].wait_recv()
    product(-1, pieces_of(-1))
    for j in range(7):
        for way in range(2):
            ring[way, j].wait_recv()
            if j + 2 < 7:
                ring[way, j + 2].start()
            hand[way, j].start()
        if j < 4:
            z_wait(0, j + 1)
            if j + 2 <= 4:
                z_ring[0, j + 2].start()
            if j < 3:
                z_wait(1, j + 1)
                if j + 2 <= 3:
                    z_ring[1, j + 2].start()
        for way in range(2):
            hand[way, j].wait_recv()
        product(j, pieces_of(j))
        if j == 4:
            over_x(0)
            over_x(1)
            for k in range(3):
                high, low = split(mats[:, k].reshape(512, 128))
                m_high[k] = high
                m_low[k] = low
    over_x(2)
    over_x(3)

    rows = []
    for k in range(NX):
        pltpu.make_async_copy(
            x_slots.at[k, pl.ds(1, NX - 1)], x_slots.at[k, pl.ds(1, NX - 1)], x_recv.at[k]
        ).wait()
        rows.append(x_slots[k, 0] + x_slots[k, 1] + x_slots[k, 2] + x_slots[k, 3])
    residual = jnp.concatenate(rows, axis=0)

    terms = dot3(residual[:, :128], m_high[0], m_low[0], 1)
    for k in range(NX):
        for h in range(4):
            t_send[4 * k + h] = terms[16 * k:16 * k + 16, 128 * h:128 * h + 128]
    sends = []
    for d in range(1, NC):
        other = (col + d) % NC
        copy = remote(
            t_send.at[other], t_slots.at[NC - d - 1], stage_send.at[0, d], stage_recv.at[0],
            at(x, z, other),
        )
        copy.start()
        sends.append(copy)
    pltpu.make_async_copy(t_slots, t_slots, stage_recv.at[0]).wait()
    total = t_send[col]
    for d in range(NC - 1):
        total = total + t_slots[d]
    s_own[...] = total
    s_full[col] = total
    for d in range(1, NC):
        other = (col + d) % NC
        copy = remote(
            s_own, s_full.at[col], stage_send.at[1, d], stage_recv.at[1], at(x, z, other)
        )
        copy.start()
        sends.append(copy)
    swap = remote(
        s_own, s_out, stage_send.at[1, 0], stage_recv.at[4], at(own_x, z, 4 * x + col % 4)
    )

    @pl.when(is_own)
    def _():
        out_one[...] = s_own[...]

    @pl.when(jnp.logical_not(is_own))
    def _():
        swap.start()

    pltpu.make_async_copy(t_slots, t_slots, stage_recv.at[1]).wait()

    solved = jnp.concatenate(
        [
            jnp.concatenate([s_full[4 * k + h] for h in range(4)], axis=1)
            for k in range(NX)
        ],
        axis=0,
    )
    coupled = dot3(solved, m_high[2], m_low[2], 0)
    c_send[...] = coupled
    for d in range(1, NX):
        copy = remote(
            c_send, c_slots.at[NX - d - 1], stage_send.at[2, d], stage_recv.at[2],
            at((x + d) % NX, z, col),
        )
        copy.start()
        sends.append(copy)
    pltpu.make_async_copy(c_slots, c_slots, stage_recv.at[2]).wait()
    second = residual[:, 128:] - coupled - c_slots[0] - c_slots[1] - c_slots[2]

    terms = dot3(second, m_high[1], m_low[1], 1)
    for k in range(NX):
        for h in range(4):
            index = 4 * k + h
            u_send[index] = terms[16 * k:16 * k + 16, 128 * h:128 * h + 128]
            mine = jnp.logical_and(x == k, col == 4 * x + h)

            @pl.when(mine)
            def _():
                pltpu.make_async_copy(
                    u_send.at[index], u_slots.at[col], stage_recv.at[3]
                ).start()

            @pl.when(jnp.logical_not(mine))
            def _():
                remote(
                    u_send.at[index], u_slots.at[col], stage_send.at[3, index],
                    stage_recv.at[3], at(k, z, 4 * x + h),
                ).start()

    pltpu.make_async_copy(u_slots, u_slots, stage_recv.at[3]).wait()
    total = u_slots[0]
    for d in range(1, NC):
        total = total + u_slots[d]
    out_two[...] = total

    @pl.when(jnp.logical_not(is_own))
    def _():
        swap.wait()
        out_one[...] = s_out[...]

    for j in range(7):
        for way in range(2):
            ring[way, j].wait_send()
            hand[way, j].wait_send()
    for half in range(2):
        hand[half, -1].wait_send()
    for copy in z_ring.values():
        copy.wait_send()
    for j in range(-1, 7):
        product_done(j, pieces_of(j))
    for q in range(4):
        over_x_done(q)
    for copy in sends:
        copy.wait_send()
    for k in range(NX):
        for h in range(4):
            index = 4 * k + h

            @pl.when(jnp.logical_not(jnp.logical_and(x == k, col == 4 * x + h)))
            def _():
                pltpu.make_async_copy(
                    u_send.at[index], u_send.at[index], stage_send.at[3, index]
                ).wait()


def per_device(
    prior_solved, block_one, block_two, cross_block, inverse_one, inverse_two, rhs_one, rhs_two
):
    vmem = pltpu.VMEM
    dma = pltpu.SemaphoreType.DMA
    out = jax.ShapeDtypeStruct((16, 128), F32)
    one, two = pl.pallas_call(
        kernel,
        out_shape=(out, out),
        in_specs=[pl.BlockSpec(memory_space=pl.ANY)] * 8,
        out_specs=(pl.BlockSpec(memory_space=pltpu.VMEM),) * 2,
        scratch_shapes=[
            vmem((2, 8, 2, 16, DEPTH), F32),
            vmem((2, 128, DEPTH), F32),
            vmem((256, DEPTH), BF16),
            vmem((256, DEPTH), BF16),
            vmem((NZ, 3, 64, 128), F32),
            vmem((3, 512, 128), BF16),
            vmem((3, 512, 128), BF16),
            vmem((2, 16, 128), F32),
            vmem((32, 16, 256), F32),
            vmem((NX, NZ, 16, 256), F32),
            vmem((4, 16, 256), F32),
            vmem((NX, NX, 16, 256), F32),
            vmem((NC, 16, 128), F32),
            vmem((NC - 1, 16, 128), F32),
            vmem((16, 128), F32),
            vmem((NC, 16, 128), F32),
            vmem((64, 128), F32),
            vmem((NX - 1, 64, 128), F32),
            vmem((NC, 16, 128), F32),
            vmem((NC, 16, 128), F32),
            vmem((16, 128), F32),
            dma((9,)),
            dma((2, 7)),
            dma((2, 7)),
            dma((2, 8)),
            dma((2, 8)),
            dma((2, 4)),
            dma((2, 4)),
            dma((32,)),
            dma((NX,)),
            dma((4, 3)),
            dma((NX,)),
            dma((4, NC)),
            dma((5,)),
        ],
        compiler_params=pltpu.CompilerParams(
            collective_id=0, has_side_effects=True, vmem_limit_bytes=40 * 1024 * 1024
        ),
    )(
        prior_solved.T, block_one, block_two, cross_block.T, inverse_one, inverse_two,
        rhs_one.T, rhs_two.T,
    )
    return one.T, two.T


def solution(mesh):
    placed = (
        P("row", "col"),
        P("col", "row"),
        P("col", "row"),
        P("col", "row"),
        P("row", "col"),
        P("row", "col"),
        P("col", "row"),
        P("col", "row"),
    )
    return jax.shard_map(
        per_device,
        mesh=mesh,
        in_specs=placed,
        out_specs=(P("col", "row"), P("col", "row")),
        check_vma=False,
    )
```

```python
import functools

import jax
import jax.numpy as jnp
from jax import lax
from jax.experimental import pallas as pl
from jax.experimental.pallas import tpu as pltpu
from jax.sharding import PartitionSpec as P

NX, NZ, NY = 4, 8, 8
Z_AT = (1, 4, 6)
DEPTH = 1536
MESH = pl.DeviceIdType.MESH
F32 = jnp.float32
BF16 = jnp.bfloat16


def split(a):
    high = a.astype(BF16)
    return high, (a - high.astype(F32)).astype(BF16)


def dot_split(a, b_high, b_low, contract):
    high = a.astype(BF16).astype(F32)
    both = jnp.concatenate([high, a - high], axis=0).astype(BF16)
    dims = (((1,), (contract,)), ((), ()))
    total = lax.dot_general(both, b_high, dims, preferred_element_type=F32)
    total = total + lax.dot_general(both, b_low, dims, preferred_element_type=F32)
    rows = a.shape[0]
    return total[:rows] + total[rows:]


def kernel(
    prior, block_one, block_two, cross, inv_one, inv_two, rhs_one, rhs_two,
    out_one, out_two,
    slab, blocks, b_high, b_low, mats, one_high, one_low, m_high, m_low, rhs,
    f_send, z_slots, x_send, x_slots, t_send, t_slots, s_own, s_full, s_mate, u_send, u_slots,
    load_sem, y_send, y_recv, mate_send, mate_recv, zr_send, zr_recv, zd_send, zd_recv, xr_send, xr_recv,
    f_sem, z_recv, x_sem, x_recv, stage_send, stage_recv,
):
    row, col = lax.axis_index("row"), lax.axis_index("col")
    x, z = row // NZ, row % NZ
    y, core = col // 2, col % 2
    other = 1 - core

    def at(xx, zz, yy, cc):
        return (NZ * xx + zz, 2 * yy + cc)

    def copy(src, dst, sem):
        return pltpu.make_async_copy(src, dst, sem)

    def remote(src, dst, send, recv, device):
        return pltpu.make_async_remote_copy(
            src_ref=src, dst_ref=dst, send_sem=send, recv_sem=recv,
            device_id=device, device_id_type=MESH,
        )

    def arrived(ref, sem):
        copy(ref, ref, sem).wait()

    own_half = slice(None)
    loads = [
        copy(inv_one, mats.at[core, 0, x, z], load_sem.at[0]),
        copy(cross, mats.at[core, 1, x, z], load_sem.at[1]),
        copy(inv_two, mats.at[core, 2, x, z], load_sem.at[2]),
        copy(block_one, blocks.at[core, pl.ds(0, 128)], load_sem.at[3]),
        copy(block_two, blocks.at[core, pl.ds(128, 128)], load_sem.at[4]),
        copy(prior.at[pl.ds(0, 16)], slab.at[7, 0], load_sem.at[5]),
        copy(prior.at[pl.ds(16, 16)], slab.at[7, 1], load_sem.at[6]),
        copy(rhs_one.at[pl.ds(pl.multiple_of(8 * core, 8), 8)], rhs.at[core, 0], load_sem.at[7]),
        copy(rhs_two.at[pl.ds(pl.multiple_of(8 * core, 8), 8)], rhs.at[core, 1], load_sem.at[8]),
    ]
    for load in loads:
        load.start()

    barrier = pltpu.get_barrier_semaphore()

    def greet(device):
        pl.semaphore_signal(barrier, inc=1, device_id=device, device_id_type=MESH)

    for d in (2, 14, 1, 4, 12, 3, 13, 5, 11, 6, 10, 7, 9, 8, 15):
        greet((row, (col + d) % 16))
    for d in range(1, NZ):
        greet(at(x, (z + d) % NZ, y, core))
    for d in range(1, NX):
        greet(at((x + d) % NX, z, y, core))
    maker = (z // 2) % 2

    @pl.when(maker != core)
    def _():
        for d in range(NZ):
            greet(at(x, (z + d) % NZ, y, maker))

    own_x = y // 2

    @pl.when(own_x != x)
    def _():
        for d in range(NY):
            greet(at(own_x, z, (y + d) % NY, core))

    pl.semaphore_wait(barrier, 15 + 7 + 3 + 4 + 6)
    makes_own = maker == core
    sums_own = own_x == x

    def half_of(way, i):
        return i % 2 if way == 0 else 1 - i % 2

    neighbours = (at(x, z, (y + 1) % NY, core), at(x, z, (y + NY - 1) % NY, core))
    ring = {}
    for way in range(2):
        for j in range(14):
            i, sub = j // 2, j % 2
            if i < 2:
                src = prior.at[pl.ds(16 * half_of(way, i) + 8 * sub, 8)]
            else:
                src = slab.at[i - 2, way, pl.ds(8 * sub, 8)]
            ring[way, j] = remote(
                src, slab.at[i, way, pl.ds(8 * sub, 8)],
                y_send, y_recv.at[way, j], neighbours[way],
            )
    for j in range(4):
        for way in range(2):
            ring[way, j].start()

    mate = at(x, z, y, other)
    other_rows = pl.ds(pl.multiple_of(8 * other, 8), 8)
    hands = [
        remote(block_one, blocks.at[core, pl.ds(0, 128)], mate_send.at[0], mate_recv.at[0], mate),
        remote(block_two, blocks.at[core, pl.ds(128, 128)], mate_send.at[1], mate_recv.at[1], mate),
        remote(rhs_one.at[other_rows], rhs.at[core, 0], mate_send.at[2], mate_recv.at[2], mate),
        remote(rhs_two.at[other_rows], rhs.at[core, 1], mate_send.at[3], mate_recv.at[3], mate),
    ]
    for hand in hands:
        hand.start()

    z_next = (at(x, (z + 1) % NZ, y, core), at(x, (z + NZ - 1) % NZ, y, core))
    order = (2, 0)

    def z_owner(way, step):
        return (z + NZ - step) % NZ if way == 0 else (z + step) % NZ

    def z_start(way, k, step):
        ref = mats.at[core, k, x, z_owner(way, step - 1)]
        remote(ref, ref, zr_send, zr_recv.at[way, k, step - 1], z_next[way]).start()

    def z_step(step):
        for k in order:
            for way in range(2):
                if step > (4, 3)[way]:
                    continue
                arrived(mats.at[core, k, x, z_owner(way, step)], zr_recv.at[way, k, step - 1])
                if step < (4, 3)[way]:
                    z_start(way, k, step + 1)

    x_next = (at((x + 1) % NX, z, y, core), at((x + 3) % NX, z, y, core))
    x_before = ((x + 3) % NX, (x + 1) % NX)

    def x_start(k):
        for way in range(2):
            ref = mats.at[core, k, x]
            remote(
                ref, ref, xr_send.at[k - 1, way, 0], xr_recv.at[k - 1, way, 0], x_next[way]
            ).start()

    def x_forward(k):
        for way in range(2):
            arrived(mats.at[core, k, x_before[way]], xr_recv.at[k - 1, way, 0])
            ref = mats.at[core, k, x_before[way], pl.ds(4 * way, 4)]
            remote(
                ref, ref, xr_send.at[k - 1, way, 1], xr_recv.at[k - 1, way, 1], x_next[way]
            ).start()

    def x_end(k):
        for way in range(2):
            arrived(mats.at[core, k, (x + 2) % NX, pl.ds(4 * way, 4)], xr_recv.at[k - 1, way, 1])
        remote(
            mats.at[core, k], mats.at[core, k], mate_send.at[4 + k], mate_recv.at[4 + k], mate
        ).start()

    def panel(k):
        arrived(mats.at[other, k], mate_recv.at[4 + k])
        for xx in range(NX):
            both = jnp.concatenate(
                [mats[c, k, xx].reshape(512, 128) for c in range(2)], axis=1
            )
            high, low = split(both)
            m_high[k - 1, 512 * xx:512 * xx + 512, :] = high
            m_low[k - 1, 512 * xx:512 * xx + 512, :] = low

    loads[1].wait()
    for d in (4, 3, 5, 2, 6, 1, 7):
        ref = mats.at[core, 1, x, z]
        remote(ref, ref, zd_send, zd_recv, at(x, (z + d) % NZ, y, core)).start()
    for k in order:
        loads[k].wait()
        for way in range(2):
            z_start(way, k, 1)

    def halves(c):
        for r in range(0, 256, 32):
            high, low = split(blocks[c, r:r + 32, :])
            b_high[c, r:r + 32, :] = high
            b_low[c, r:r + 32, :] = low

    def owner_of(i, way):
        if i == 7:
            py, half = y, way
        else:
            step = i // 2 + 1
            py = (y + NY - step) % NY if way == 0 else (y + step) % NY
            half = half_of(way, i)
        return py // 2, 4 * (py % 2) + 2 * core + half

    def product(i):
        a = slab[i].reshape(32, DEPTH)
        f = dot_split(
            a, b_high[...].reshape(512, DEPTH), b_low[...].reshape(512, DEPTH), 1
        )
        for way in range(2):
            owner_x, owner_z = owner_of(i, way)
            slot = z_slots.at[owner_x, (z - owner_z + NZ) % NZ]
            for c in range(2):
                index = 4 * i + 2 * way + c
                r = 16 * way + 8 * c
                f_send[index] = f[r:r + 8, :]
                mine = jnp.logical_and(owner_z == z, core == c)

                @pl.when(mine)
                def _():
                    copy(f_send.at[index], slot, z_recv.at[owner_x]).start()

                @pl.when(jnp.logical_not(mine))
                def _():
                    remote(
                        f_send.at[index], slot, f_sem, z_recv.at[owner_x],
                        at(x, owner_z, y, c),
                    ).start()

    odd = jnp.where(y % 2 == z // 4, 0, 1)

    def over_x(q):
        shift = (0 + odd, 2 - 3 * odd, -2 + 5 * odd, 4 - 7 * odd)[q]
        which = ((y + shift + NY) % NY) // 2
        arrived(z_slots.at[which], z_recv.at[which])
        total = z_slots[which, 0]
        for d in range(1, NZ):
            total = total + z_slots[which, d]
        mine = jnp.where(which == x, 1.0, 0.0).astype(F32)
        given = jnp.concatenate([rhs[0, 0], rhs[0, 1], rhs[1, 0], rhs[1, 1]], axis=1)
        part = given * mine - total
        x_slots[which, 0] = part
        x_send[q] = part
        for d in (2, 1, 3):
            remote(
                x_send.at[q], x_slots.at[which, NX - d], x_sem, x_recv,
                at((x + d) % NX, z, y, core),
            ).start()

    for i in range(7):
        for sub in range(2):
            j = 2 * i + sub
            for way in range(2):
                ring[way, j].wait_recv()
                if j + 4 < 14:
                    ring[way, j + 4].start()
            if j == 0:
                for load in loads[3:]:
                    load.wait()
                halves(core)
            if j == 1:
                for hand in hands[:2]:
                    hand.wait_recv()
                halves(other)
            if j == 2:
                product(7)
            if j == 3:
                product(0)
            if sub == 0 and i >= 2:
                product(i - 1)
        if i in Z_AT:
            z_step(Z_AT.index(i) + 1)
        if i == 3:
            arrived(mats.at[core, 1, x, pl.ds(0, 7)], zd_recv)
            x_start(1)
    product(6)
    x_forward(1)
    z_step(4)
    x_start(2)
    remote(
        mats.at[core, 0, x], mats.at[core, 0, x], mate_send.at[4], mate_recv.at[4], mate
    ).start()
    for hand in hands[2:]:
        hand.wait_recv()
    for q in range(3):
        over_x(q)
    arrived(mats.at[other, 0, x], mate_recv.at[4])
    both = jnp.concatenate([mats[c, 0, x].reshape(512, 128) for c in range(2)], axis=1)
    high, low = split(both)
    one_high[...] = high
    one_low[...] = low
    over_x(3)
    x_end(1)

    arrived(x_slots.at[pl.ds(0, 3)], x_recv)

    def residual(k):
        return x_slots[k, 0] + x_slots[k, 1] + x_slots[k, 2] + x_slots[k, 3]

    def of_block(b, r):
        return jnp.concatenate(
            [r[:, 128 * b:128 * b + 128], r[:, 256 + 128 * b:384 + 128 * b]], axis=1
        )

    first = jnp.concatenate([of_block(0, residual(k)) for k in range(NX)], axis=0)

    terms = dot_split(first, one_high[...], one_low[...], 1)
    for k in range(NX):
        for e in range(2):
            index = 2 * k + e
            t_send[index] = terms[8 * k:8 * k + 8, 256 * e:256 * e + 256]
            mine = jnp.logical_and(x == k, y == 2 * x + e)

            @pl.when(mine)
            def _():
                copy(t_send.at[index], t_slots.at[y], stage_recv.at[0]).start()

            @pl.when(jnp.logical_not(mine))
            def _():
                remote(
                    t_send.at[index], t_slots.at[y], stage_send.at[0], stage_recv.at[0],
                    at(k, z, 2 * x + e, core),
                ).start()

    x_forward(2)
    panel(1)
    second = of_block(1, residual(x))
    arrived(t_slots, stage_recv.at[0])
    total = t_slots[0]
    for d in range(1, NY):
        total = total + t_slots[d]
    s_own[...] = total
    s_full[y] = total
    for d in (4, 3, 5, 2, 6, 1, 7):
        remote(
            s_own, s_full.at[y], stage_send.at[1], stage_recv.at[1],
            at(x, z, (y + d) % NY, core),
        ).start()
    s_mate[0] = total[:, :128]
    s_mate[1] = total[:, 128:]
    swap = remote(
        s_mate.at[other], s_mate.at[2], mate_send.at[7], mate_recv.at[7], mate
    )
    swap.start()
    x_end(2)
    swap.wait()
    out_one[pl.ds(pl.multiple_of(8 * core, 8), 8), :] = s_mate[core]
    out_one[pl.ds(pl.multiple_of(8 * other, 8), 8), :] = s_mate[2]

    arrived(slab.at[pl.ds(0, 7)], y_send)
    for hand in hands:
        hand.wait_send()
    arrived(mats.at[core, 0, x], mate_send.at[4])
    arrived(mats.at[core, pl.ds(0, 2), 0, pl.ds(0, 7)], zr_send)
    arrived(mats.at[core, 0, 0, pl.ds(0, 7)], zd_send)
    for k in range(1, 3):
        for way in range(2):
            arrived(mats.at[core, k, x], xr_send.at[k - 1, way, 0])
            arrived(mats.at[core, k, x, pl.ds(0, 4)], xr_send.at[k - 1, way, 1])
        arrived(mats.at[core, k], mate_send.at[4 + k])

    @pl.when(makes_own)
    def _():
        arrived(f_send.at[pl.ds(0, 28)], f_sem)

    @pl.when(jnp.logical_not(makes_own))
    def _():
        arrived(f_send, f_sem)

    arrived(x_slots.at[pl.ds(0, 3)], x_sem)

    @pl.when(sums_own)
    def _():
        arrived(t_send.at[pl.ds(0, 7)], stage_send.at[0])

    @pl.when(jnp.logical_not(sums_own))
    def _():
        arrived(t_send, stage_send.at[0])

    panel(2)

    arrived(s_full.at[pl.ds(0, 7)], stage_recv.at[1])
    solved = jnp.concatenate([s_full[k] for k in range(NY)], axis=1)
    second = second - dot_split(solved, m_high[0], m_low[0], 0)

    terms = dot_split(second, m_high[1], m_low[1], 1)
    for k in range(16):
        u_send[k] = terms[:, 128 * k:128 * k + 128]
    u_slots[8 * core + y] = u_send[col]
    for d in (8, 9, 7, 6, 10, 5, 11, 4, 12, 3, 13, 2, 14, 1, 15):
        to = (col + d) % 16
        remote(
            u_send.at[to], u_slots.at[8 * core + y], stage_send.at[2], stage_recv.at[2],
            (row, to),
        ).start()
    arrived(s_full.at[pl.ds(0, 7)], stage_send.at[1])
    arrived(u_slots.at[pl.ds(0, 15)], stage_recv.at[2])
    for half in range(2):
        total = u_slots[8 * half]
        for d in range(1, NY):
            total = total + u_slots[8 * half + d]
        out_two[8 * half:8 * half + 8, :] = total
    arrived(u_slots.at[pl.ds(0, 15)], stage_send.at[2])


def per_device(
    prior_solved, block_one, block_two, cross_block, inverse_one, inverse_two, rhs_one, rhs_two
):
    vmem = pltpu.VMEM
    dma = pltpu.SemaphoreType.DMA
    out = jax.ShapeDtypeStruct((16, 128), F32)
    one, two = pl.pallas_call(
        kernel,
        out_shape=(out, out),
        in_specs=[pl.BlockSpec(memory_space=pltpu.HBM)] * 8,
        out_specs=(pl.BlockSpec(memory_space=pltpu.VMEM),) * 2,
        scratch_shapes=[
            vmem((8, 2, 16, DEPTH), F32),
            vmem((2, 256, DEPTH), F32),
            vmem((2, 256, DEPTH), BF16),
            vmem((2, 256, DEPTH), BF16),
            vmem((2, 3, NX, NZ, 64, 128), F32),
            vmem((512, 256), BF16),
            vmem((512, 256), BF16),
            vmem((2, 2048, 256), BF16),
            vmem((2, 2048, 256), BF16),
            vmem((2, 2, 8, 128), F32),
            vmem((32, 8, 512), F32),
            vmem((NX, NZ, 8, 512), F32),
            vmem((4, 8, 512), F32),
            vmem((NX, NX, 8, 512), F32),
            vmem((8, 8, 256), F32),
            vmem((NY, 8, 256), F32),
            vmem((8, 256), F32),
            vmem((NY, 8, 256), F32),
            vmem((3, 8, 128), F32),
            vmem((16, 8, 128), F32),
            vmem((16, 8, 128), F32),
            dma((9,)),
            dma,
            dma((2, 14)),
            dma((8,)),
            dma((8,)),
            dma,
            dma((2, 3, 4)),
            dma,
            dma,
            dma((2, 2, 2)),
            dma((2, 2, 2)),
            dma,
            dma((NX,)),
            dma,
            dma,
            dma((3,)),
            dma((3,)),
        ],
        compiler_params=pltpu.CompilerParams(
            collective_id=0, has_side_effects=True, vmem_limit_bytes=62 * 1024 * 1024
        ),
    )(
        prior_solved.T, block_one, block_two, cross_block.T, inverse_one, inverse_two,
        rhs_one.T, rhs_two.T,
    )
    return one.T, two.T


def solution(mesh):
    placed = (
        P("row", "col"),
        P("col", "row"),
        P("col", "row"),
        P("col", "row"),
        P("row", "col"),
        P("row", "col"),
        P("col", "row"),
        P("col", "row"),
    )
    return jax.shard_map(
        per_device,
        mesh=mesh,
        in_specs=placed,
        out_specs=(P("col", "row"), P("col", "row")),
        check_vma=False,
    )
```

```python
import functools

import jax
import jax.numpy as jnp
from jax import lax
from jax.experimental import pallas as pl
from jax.experimental.pallas import tpu as pltpu
from jax.sharding import PartitionSpec as P

NX, NZ, NY = 4, 8, 8
C_AT = 0
X_AT = (3, 5)
RING_AT = (2, 5, 6)
DEPTH = 1536
MESH = pl.DeviceIdType.MESH
F32 = jnp.float32
BF16 = jnp.bfloat16


def split(a):
    high = a.astype(BF16)
    return high, (a - high.astype(F32)).astype(BF16)


def dot_split(a, b_high, b_low, contract):
    high = a.astype(BF16).astype(F32)
    both = jnp.concatenate([high, a - high], axis=0).astype(BF16)
    dims = (((1,), (contract,)), ((), ()))
    total = lax.dot_general(both, b_high, dims, preferred_element_type=F32)
    total = total + lax.dot_general(both, b_low, dims, preferred_element_type=F32)
    rows = a.shape[0]
    return total[:rows] + total[rows:]


def kernel(
    prior, block_one, block_two, cross, inv_one, inv_two, rhs_one, rhs_two,
    out,
    slab, blocks, b_high, b_low, mats, m_high, m_low, rhs,
    f_send, x_slots, q_send, z_slots, t_send, t_slots, s_own, s_full, s_mate, u_send, u_slots,
    load_sem, y_send, y_recv, mate_send, mate_recv, zd_send, zd_recv, xd_send, xd_recv, zr_send, zr_recv, xr_send, xr_recv,
    f_sem, f_recv, q_sem, q_recv, stage_send, stage_recv,
):
    row, col = lax.axis_index("row"), lax.axis_index("col")
    x, z = row // NZ, row % NZ
    y, core = col // 2, col % 2
    other = 1 - core

    def at(xx, zz, yy, cc):
        return (NZ * xx + zz, 2 * yy + cc)

    def copy(src, dst, sem):
        return pltpu.make_async_copy(src, dst, sem)

    def remote(src, dst, send, recv, device):
        return pltpu.make_async_remote_copy(
            src_ref=src, dst_ref=dst, send_sem=send, recv_sem=recv,
            device_id=device, device_id_type=MESH,
        )

    def arrived(ref, sem):
        copy(ref, ref, sem).wait()

    own_half = slice(None)
    loads = [
        copy(inv_one, mats.at[core, 0, x, z], load_sem.at[0]),
        copy(cross, mats.at[core, 1, x, z], load_sem.at[1]),
        copy(inv_two, mats.at[core, 2, x, z], load_sem.at[2]),
        copy(block_one, blocks.at[core, pl.ds(0, 128)], load_sem.at[3]),
        copy(block_two, blocks.at[core, pl.ds(128, 128)], load_sem.at[4]),
        copy(prior.at[pl.ds(0, 16)], slab.at[7, 0], load_sem.at[5]),
        copy(prior.at[pl.ds(16, 16)], slab.at[7, 1], load_sem.at[6]),
        copy(rhs_one.at[pl.ds(pl.multiple_of(8 * core, 8), 8)], rhs.at[core, 0], load_sem.at[7]),
        copy(rhs_two.at[pl.ds(pl.multiple_of(8 * core, 8), 8)], rhs.at[core, 1], load_sem.at[8]),
    ]
    for load in loads:
        load.start()

    barrier = pltpu.get_barrier_semaphore()

    def greet(device):
        pl.semaphore_signal(barrier, inc=1, device_id=device, device_id_type=MESH)

    for d in (2, 14, 1, 4, 12, 3, 13, 5, 11, 6, 10, 7, 9, 8, 15):
        greet((row, (col + d) % 16))
    for d in range(1, NZ):
        greet(at(x, (z + d) % NZ, y, core))
    for d in range(1, NX):
        for c in range(2):
            greet(at((x + d) % NX, z, y, c))
    pl.semaphore_wait(barrier, 15 + 7 + 6)

    def half_of(way, i):
        return i % 2 if way == 0 else 1 - i % 2

    neighbours = (at(x, z, (y + 1) % NY, core), at(x, z, (y + NY - 1) % NY, core))
    ring = {}
    for way in range(2):
        for j in range(14):
            i, sub = j // 2, j % 2
            if i < 2:
                src = prior.at[pl.ds(16 * half_of(way, i) + 8 * sub, 8)]
            else:
                src = slab.at[i - 2, way, pl.ds(8 * sub, 8)]
            ring[way, j] = remote(
                src, slab.at[i, way, pl.ds(8 * sub, 8)],
                y_send, y_recv.at[way, j], neighbours[way],
            )
    for j in range(4):
        for way in range(2):
            ring[way, j].start()

    mate = at(x, z, y, other)
    other_rows = pl.ds(pl.multiple_of(8 * other, 8), 8)
    hands = [
        remote(block_one, blocks.at[core, pl.ds(0, 128)], mate_send.at[0], mate_recv.at[0], mate),
        remote(block_two, blocks.at[core, pl.ds(128, 128)], mate_send.at[1], mate_recv.at[1], mate),
        remote(rhs_one.at[other_rows], rhs.at[core, 0], mate_send.at[2], mate_recv.at[2], mate),
        remote(rhs_two.at[other_rows], rhs.at[core, 1], mate_send.at[3], mate_recv.at[3], mate),
    ]
    for hand in hands:
        hand.start()

    def z_start(k):
        loads[k].wait()
        for d in (4, 3, 5, 2, 6, 1, 7):
            ref = mats.at[core, k, x, z]
            remote(
                ref, ref, zd_send, zd_recv.at[k], at(x, (z + d) % NZ, y, core)
            ).start()

    def z_end(k):
        arrived(mats.at[core, k, x, pl.ds(0, 7)], zd_recv.at[k])

    def two_start():
        loads[2].wait()
        ref = mats.at[core, 2, x, z]
        for d in (2, 1, 3):
            remote(ref, ref, xd_send, xd_recv, at((x + d) % NX, z, y, core)).start()

    z_next = (at(x, (z + 1) % NZ, y, core), at(x, (z + NZ - 1) % NZ, y, core))

    def two_step(step):
        if step == 0:
            arrived(mats.at[core, 2, pl.ds(0, 3), z], xd_recv)
        for way in range(2):
            last = (4, 3)[way]
            owner = (z + NZ - step) % NZ if way == 0 else (z + step) % NZ
            ref = mats.at[core, 2, pl.ds(0, NX), owner]
            if 0 < step <= last:
                arrived(ref, zr_recv.at[way, step - 1])
            if step < last:
                remote(ref, ref, zr_send, zr_recv.at[way, step], z_next[way]).start()

    x_next = (at((x + 1) % NX, z, y, core), at((x + 3) % NX, z, y, core))
    x_before = ((x + 3) % NX, (x + 1) % NX)

    def x_start(k):
        for way in range(2):
            ref = mats.at[core, k, x]
            remote(
                ref, ref, xr_send.at[k, way, 0], xr_recv.at[k, way, 0], x_next[way]
            ).start()

    def x_forward(k):
        for way in range(2):
            arrived(mats.at[core, k, x_before[way]], xr_recv.at[k, way, 0])
            ref = mats.at[core, k, x_before[way], pl.ds(4 * way, 4)]
            remote(
                ref, ref, xr_send.at[k, way, 1], xr_recv.at[k, way, 1], x_next[way]
            ).start()

    def to_mate(k):
        remote(
            mats.at[core, k], mats.at[core, k], mate_send.at[4 + k], mate_recv.at[4 + k], mate
        ).start()

    def x_end(k):
        for way in range(2):
            arrived(mats.at[core, k, (x + 2) % NX, pl.ds(4 * way, 4)], xr_recv.at[k, way, 1])
        to_mate(k)

    def panel_rows(k, xx):
        both = jnp.concatenate(
            [mats[c, k, xx].reshape(512, 128) for c in range(2)], axis=1
        )
        high, low = split(both)
        m_high[k, xx] = high
        m_low[k, xx] = low

    def panel(k):
        arrived(mats.at[other, k], mate_recv.at[4 + k])
        for xx in range(NX):
            panel_rows(k, xx)

    def one_to_mate(d, sem):
        ref = mats.at[core, 0, (x + d) % NX]
        remote(ref, ref, mate_send.at[sem], mate_recv.at[sem], mate).start()

    def one_near():
        arrived(mats.at[other, 0, pl.ds(0, 3)], mate_recv.at[4])
        for d in (0, 1, 3):
            panel_rows(0, (x + d) % NX)

    def one_far():
        for way in range(2):
            arrived(mats.at[core, 0, (x + 2) % NX, pl.ds(4 * way, 4)], xr_recv.at[0, way, 1])
        one_to_mate(2, 8)
        arrived(mats.at[other, 0, (x + 2) % NX], mate_recv.at[8])
        panel_rows(0, (x + 2) % NX)

    z_start(0)
    two_start()

    def halves(c):
        for r in range(0, 256, 32):
            high, low = split(blocks[c, r:r + 32, :])
            b_high[c, r:r + 32, :] = high
            b_low[c, r:r + 32, :] = low

    def owner_of(i, way):
        if i == 7:
            py, half = y, way
        else:
            step = i // 2 + 1
            py = (y + NY - step) % NY if way == 0 else (y + step) % NY
            half = half_of(way, i)
        return py // 2, 4 * (py % 2) + 2 * core + half

    def product(i):
        a = slab[i].reshape(32, DEPTH)
        f = dot_split(
            a, b_high[...].reshape(512, DEPTH), b_low[...].reshape(512, DEPTH), 1
        )
        for way in range(2):
            owner_x, owner_z = owner_of(i, way)
            slot = x_slots.at[owner_z, (x - owner_x + NX) % NX]
            for c in range(2):
                index = 4 * i + 2 * way + c
                r = 16 * way + 8 * c
                f_send[index] = f[r:r + 8, :]
                mine = jnp.logical_and(owner_x == x, core == c)

                @pl.when(mine)
                def _():
                    copy(f_send.at[index], slot, f_recv.at[owner_z]).start()

                @pl.when(jnp.logical_not(mine))
                def _():
                    remote(
                        f_send.at[index], slot, f_sem, f_recv.at[owner_z],
                        at(owner_x, z, y, c),
                    ).start()

    def apart(a):
        return jnp.minimum((a - y + NY) % NY, (y - a + NY) % NY)

    far = jnp.where(apart(2 * x) > apart(2 * x + 1), 0, 1)

    def over_z(which):
        arrived(x_slots.at[which], f_recv.at[which])
        total = x_slots[which, 0]
        for d in range(1, NX):
            total = total + x_slots[which, d]

        @pl.when(which == z)
        def _():
            z_slots[0] = total

        @pl.when(which != z)
        def _():
            q_send[which] = total
            remote(
                q_send.at[which], z_slots.at[(z - which + NZ) % NZ], q_sem, q_recv,
                at(x, which, y, core),
            ).start()

    for i in range(7):
        for sub in range(2):
            j = 2 * i + sub
            for way in range(2):
                ring[way, j].wait_recv()
                if j + 4 < 14:
                    ring[way, j + 4].start()
            if j == 0:
                for load in loads[3:]:
                    load.wait()
                halves(core)
            if j == 1:
                for hand in hands[:2]:
                    hand.wait_recv()
                halves(other)
            if j == 2:
                product(7)
            if j == 3:
                product(0)
            if sub == 0 and i >= 2:
                product(i - 1)
        if i == C_AT:
            z_start(1)
        if i in RING_AT:
            two_step(RING_AT.index(i))
        if i in X_AT:
            z_end(X_AT.index(i))
            x_start(X_AT.index(i))
    product(6)
    x_forward(0)
    for d in (0, 1, 3):
        one_to_mate(d, 4)
    for hand in hands[2:]:
        hand.wait_recv()
    for t in range(4):
        over_z(4 * (1 - far) + t)
    for t in range(4):
        over_z(4 * far + t)
    two_step(3)
    one_near()
    x_forward(1)
    one_far()

    arrived(z_slots.at[pl.ds(1, NZ - 1)], q_recv)
    total = z_slots[0]
    for d in range(1, NZ):
        total = total + z_slots[d]
    residual = (
        jnp.concatenate([rhs[0, 0], rhs[0, 1], rhs[1, 0], rhs[1, 1]], axis=1) - total
    )

    def weights(ref, k):
        return ref[k].reshape(2048, 256)

    def of_block(b):
        return jnp.concatenate(
            [residual[:, 128 * b:128 * b + 128], residual[:, 256 + 128 * b:384 + 128 * b]], axis=1
        )

    terms = dot_split(of_block(0), weights(m_high, 0), weights(m_low, 0), 1)
    for k in range(NY):
        t_send[k] = terms[:, 256 * k:256 * k + 256]
    for d in (4, 3, 5, 2, 6, 1, 7):
        to = (y + d) % NY
        remote(
            t_send.at[to], t_slots.at[NY - 1 - d], stage_send.at[0], stage_recv.at[0],
            at(x, z, to, core),
        ).start()

    x_end(1)
    two_step(4)
    to_mate(2)
    second = of_block(1)
    arrived(t_slots, stage_recv.at[0])
    total = t_send[y]
    for d in range(NY - 1):
        total = total + t_slots[d]
    s_own[...] = total
    s_full[y] = total
    for d in (4, 3, 5, 2, 6, 1, 7):
        remote(
            s_own, s_full.at[y], stage_send.at[1], stage_recv.at[1],
            at(x, z, (y + d) % NY, core),
        ).start()
    s_mate[0] = total[:, :128]
    s_mate[1] = total[:, 128:]
    swap = remote(
        s_mate.at[other], s_mate.at[2], mate_send.at[7], mate_recv.at[7], mate
    )
    swap.start()
    panel(1)
    swap.wait()
    out[0, pl.ds(pl.multiple_of(8 * core, 8), 8), :] = s_mate[core]
    out[0, pl.ds(pl.multiple_of(8 * other, 8), 8), :] = s_mate[2]

    arrived(slab.at[pl.ds(0, 7)], y_send)
    for hand in hands:
        hand.wait_send()
    arrived(mats.at[core, pl.ds(0, 2), 0, pl.ds(0, 7)], zd_send)
    arrived(mats.at[core, 2, pl.ds(0, 3), 0], xd_send)
    arrived(mats.at[core, 2, pl.ds(0, 4), pl.ds(0, 7)], zr_send)
    for k in range(2):
        for way in range(2):
            arrived(mats.at[core, k, x], xr_send.at[k, way, 0])
            arrived(mats.at[core, k, x, pl.ds(0, 4)], xr_send.at[k, way, 1])
    arrived(mats.at[core, 0, pl.ds(0, 3)], mate_send.at[4])
    arrived(mats.at[core, 0, 0], mate_send.at[8])
    for k in range(1, 3):
        arrived(mats.at[core, k], mate_send.at[4 + k])
    arrived(f_send.at[pl.ds(0, 28)], f_sem)
    arrived(q_send.at[pl.ds(0, 7)], q_sem)
    arrived(t_slots, stage_send.at[0])
    panel(2)

    arrived(s_full.at[pl.ds(0, 7)], stage_recv.at[1])
    solved = jnp.concatenate([s_full[k] for k in range(NY)], axis=1)
    second = second - dot_split(solved, weights(m_high, 1), weights(m_low, 1), 0)

    terms = dot_split(second, weights(m_high, 2), weights(m_low, 2), 1)
    for k in range(16):
        u_send[k] = terms[:, 128 * k:128 * k + 128]
    u_slots[8 * core + y] = u_send[col]
    for d in (8, 9, 7, 6, 10, 5, 11, 4, 12, 3, 13, 2, 14, 1, 15):
        to = (col + d) % 16
        remote(
            u_send.at[to], u_slots.at[8 * core + y], stage_send.at[2], stage_recv.at[2],
            (row, to),
        ).start()
    arrived(s_full.at[pl.ds(0, 7)], stage_send.at[1])
    arrived(u_slots.at[pl.ds(0, 15)], stage_recv.at[2])
    for half in range(2):
        total = u_slots[8 * half]
        for d in range(1, NY):
            total = total + u_slots[8 * half + d]
        out[1, 8 * half:8 * half + 8, :] = total
    arrived(u_slots.at[pl.ds(0, 15)], stage_send.at[2])


def per_device(
    prior_solved, block_one, block_two, cross_block, inverse_one, inverse_two, rhs_one, rhs_two
):
    vmem = pltpu.VMEM
    dma = pltpu.SemaphoreType.DMA
    out = pl.pallas_call(
        kernel,
        out_shape=jax.ShapeDtypeStruct((2, 16, 128), F32),
        in_specs=[pl.BlockSpec(memory_space=pltpu.HBM)] * 8,
        out_specs=pl.BlockSpec(memory_space=pltpu.VMEM),
        scratch_shapes=[
            vmem((8, 2, 16, DEPTH), F32),
            vmem((2, 256, DEPTH), F32),
            vmem((2, 256, DEPTH), BF16),
            vmem((2, 256, DEPTH), BF16),
            vmem((2, 3, NX, NZ, 64, 128), F32),
            vmem((3, NX, 512, 256), BF16),
            vmem((3, NX, 512, 256), BF16),
            vmem((2, 2, 8, 128), F32),
            vmem((32, 8, 512), F32),
            vmem((NZ, NX, 8, 512), F32),
            vmem((NZ, 8, 512), F32),
            vmem((NZ, 8, 512), F32),
            vmem((NY, 8, 256), F32),
            vmem((NY - 1, 8, 256), F32),
            vmem((8, 256), F32),
            vmem((NY, 8, 256), F32),
            vmem((3, 8, 128), F32),
            vmem((16, 8, 128), F32),
            vmem((16, 8, 128), F32),
            dma((9,)),
            dma,
            dma((2, 14)),
            dma((9,)),
            dma((9,)),
            dma,
            dma((2,)),
            dma,
            dma,
            dma,
            dma((2, 4)),
            dma((2, 2, 2)),
            dma((2, 2, 2)),
            dma,
            dma((NZ,)),
            dma,
            dma,
            dma((3,)),
            dma((3,)),
        ],
        compiler_params=pltpu.CompilerParams(
            collective_id=0, has_side_effects=True, vmem_limit_bytes=62 * 1024 * 1024
        ),
    )(
        prior_solved.T, block_one, block_two, cross_block.T, inverse_one, inverse_two,
        rhs_one.T, rhs_two.T,
    )
    return out[0].T, out[1].T


def solution(mesh):
    placed = (
        P("row", "col"),
        P("col", "row"),
        P("col", "row"),
        P("col", "row"),
        P("row", "col"),
        P("row", "col"),
        P("col", "row"),
        P("col", "row"),
    )
    return jax.shard_map(
        per_device,
        mesh=mesh,
        in_specs=placed,
        out_specs=(P("col", "row"), P("col", "row")),
        check_vma=False,
    )
```

```python
import functools

import jax
import jax.numpy as jnp
from jax import lax
from jax.experimental import pallas as pl
from jax.experimental.pallas import tpu as pltpu
from jax.sharding import PartitionSpec as P

NX, NZ, NY = 4, 8, 8
X_AT = 3
RING_AT = ((0, 3, 5), (0, 4, 6))
DEPTH = 1536
MESH = pl.DeviceIdType.MESH
F32 = jnp.float32
BF16 = jnp.bfloat16


def split(a):
    high = a.astype(BF16)
    return high, (a - high.astype(F32)).astype(BF16)


def dot_split(a, b_high, b_low, contract):
    high = a.astype(BF16).astype(F32)
    both = jnp.concatenate([high, a - high], axis=0).astype(BF16)
    dims = (((1,), (contract,)), ((), ()))
    total = lax.dot_general(both, b_high, dims, preferred_element_type=F32)
    total = total + lax.dot_general(both, b_low, dims, preferred_element_type=F32)
    rows = a.shape[0]
    return total[:rows] + total[rows:]


def kernel(
    prior, block_one, block_two, cross, inv_one, inv_two, rhs_one, rhs_two,
    out,
    slab, blocks, b_high, b_low, mats, m_high, m_low, rhs,
    f_send, x_slots, q_send, z_slots, t_send, t_slots, s_own, s_full, s_mate, u_send, u_slots,
    load_sem, y_send, y_recv, mate_send, mate_recv, zd_send, zd_recv, xd_send, xd_recv, zr_send, zr_recv, xr_send, xr_recv,
    f_sem, f_recv, q_sem, q_recv, stage_send, stage_recv,
):
    row, col = lax.axis_index("row"), lax.axis_index("col")
    x, z = row // NZ, row % NZ
    y, core = col // 2, col % 2
    other = 1 - core

    def at(xx, zz, yy, cc):
        return (NZ * xx + zz, 2 * yy + cc)

    def copy(src, dst, sem):
        return pltpu.make_async_copy(src, dst, sem)

    def remote(src, dst, send, recv, device):
        return pltpu.make_async_remote_copy(
            src_ref=src, dst_ref=dst, send_sem=send, recv_sem=recv,
            device_id=device, device_id_type=MESH,
        )

    def arrived(ref, sem):
        copy(ref, ref, sem).wait()

    own_half = slice(None)
    loads = [
        copy(inv_one, mats.at[core, 0, x, z], load_sem.at[0]),
        copy(cross, mats.at[core, 1, x, z], load_sem.at[1]),
        copy(inv_two, mats.at[core, 2, x, z], load_sem.at[2]),
        copy(block_one, blocks.at[core, pl.ds(0, 128)], load_sem.at[3]),
        copy(block_two, blocks.at[core, pl.ds(128, 128)], load_sem.at[4]),
        copy(prior.at[pl.ds(0, 16)], slab.at[7, 0], load_sem.at[5]),
        copy(prior.at[pl.ds(16, 16)], slab.at[7, 1], load_sem.at[6]),
        copy(rhs_one.at[pl.ds(pl.multiple_of(8 * core, 8), 8)], rhs.at[core, 0], load_sem.at[7]),
        copy(rhs_two.at[pl.ds(pl.multiple_of(8 * core, 8), 8)], rhs.at[core, 1], load_sem.at[8]),
    ]
    for load in loads:
        load.start()

    barrier = pltpu.get_barrier_semaphore()

    def greet(device):
        pl.semaphore_signal(barrier, inc=1, device_id=device, device_id_type=MESH)

    for d in (2, 14, 1, 4, 12, 3, 13, 5, 11, 6, 10, 7, 9, 8, 15):
        greet((row, (col + d) % 16))
    for d in range(1, NZ):
        greet(at(x, (z + d) % NZ, y, core))
    for d in range(1, NX):
        for c in range(2):
            greet(at((x + d) % NX, z, y, c))
    pl.semaphore_wait(barrier, 15 + 7 + 6)

    def half_of(way, i):
        return i % 2 if way == 0 else 1 - i % 2

    neighbours = (at(x, z, (y + 1) % NY, core), at(x, z, (y + NY - 1) % NY, core))
    ring = {}
    for way in range(2):
        for j in range(14):
            i, sub = j // 2, j % 2
            if i < 2:
                src = prior.at[pl.ds(16 * half_of(way, i) + 8 * sub, 8)]
            else:
                src = slab.at[i - 2, way, pl.ds(8 * sub, 8)]
            ring[way, j] = remote(
                src, slab.at[i, way, pl.ds(8 * sub, 8)],
                y_send, y_recv.at[way, j], neighbours[way],
            )
    for j in range(4):
        for way in range(2):
            ring[way, j].start()

    mate = at(x, z, y, other)
    other_rows = pl.ds(pl.multiple_of(8 * other, 8), 8)
    hands = [
        remote(block_one, blocks.at[core, pl.ds(0, 128)], mate_send.at[0], mate_recv.at[0], mate),
        remote(block_two, blocks.at[core, pl.ds(128, 128)], mate_send.at[1], mate_recv.at[1], mate),
        remote(rhs_one.at[other_rows], rhs.at[core, 0], mate_send.at[2], mate_recv.at[2], mate),
        remote(rhs_two.at[other_rows], rhs.at[core, 1], mate_send.at[3], mate_recv.at[3], mate),
    ]
    for hand in hands:
        hand.start()

    def z_start(k):
        loads[k].wait()
        for d in (4, 3, 5, 2, 6, 1, 7):
            ref = mats.at[core, k, x, z]
            remote(
                ref, ref, zd_send, zd_recv.at[k], at(x, (z + d) % NZ, y, core)
            ).start()

    def z_end(k):
        arrived(mats.at[core, k, x, pl.ds(0, 7)], zd_recv.at[k])

    def ring_start(k):
        loads[k].wait()
        ref = mats.at[core, k, x, z]
        for d in (2, 1, 3):
            remote(
                ref, ref, xd_send, xd_recv.at[k - 1], at((x + d) % NX, z, y, core)
            ).start()

    z_next = (at(x, (z + 1) % NZ, y, core), at(x, (z + NZ - 1) % NZ, y, core))

    def ring_step(k, step):
        if step == 0:
            arrived(mats.at[core, k, pl.ds(0, 3), z], xd_recv.at[k - 1])
        for way in range(2):
            last = (4, 3)[way]
            owner = (z + NZ - step) % NZ if way == 0 else (z + step) % NZ
            ref = mats.at[core, k, pl.ds(0, NX), owner]
            if 0 < step <= last:
                arrived(ref, zr_recv.at[k - 1, way, step - 1])
            if step < last:
                remote(ref, ref, zr_send, zr_recv.at[k - 1, way, step], z_next[way]).start()

    x_next = (at((x + 1) % NX, z, y, core), at((x + 3) % NX, z, y, core))
    x_before = ((x + 3) % NX, (x + 1) % NX)

    def x_start(k):
        for way in range(2):
            ref = mats.at[core, k, x]
            remote(
                ref, ref, xr_send.at[k, way, 0], xr_recv.at[k, way, 0], x_next[way]
            ).start()

    def x_forward(k):
        for way in range(2):
            arrived(mats.at[core, k, x_before[way]], xr_recv.at[k, way, 0])
            ref = mats.at[core, k, x_before[way], pl.ds(4 * way, 4)]
            remote(
                ref, ref, xr_send.at[k, way, 1], xr_recv.at[k, way, 1], x_next[way]
            ).start()

    def to_mate(k):
        remote(
            mats.at[core, k], mats.at[core, k], mate_send.at[4 + k], mate_recv.at[4 + k], mate
        ).start()

    def panel_rows(k, xx):
        both = jnp.concatenate(
            [mats[c, k, xx].reshape(512, 128) for c in range(2)], axis=1
        )
        high, low = split(both)
        m_high[k, xx] = high
        m_low[k, xx] = low

    def panel(k):
        arrived(mats.at[other, k], mate_recv.at[4 + k])
        for xx in range(NX):
            panel_rows(k, xx)

    def one_to_mate(d, sem):
        ref = mats.at[core, 0, (x + d) % NX]
        remote(ref, ref, mate_send.at[sem], mate_recv.at[sem], mate).start()

    def one_near():
        arrived(mats.at[other, 0, pl.ds(0, 3)], mate_recv.at[4])
        for d in (0, 1, 3):
            panel_rows(0, (x + d) % NX)

    def one_far():
        for way in range(2):
            arrived(mats.at[core, 0, (x + 2) % NX, pl.ds(4 * way, 4)], xr_recv.at[0, way, 1])
        one_to_mate(2, 8)
        arrived(mats.at[other, 0, (x + 2) % NX], mate_recv.at[8])
        panel_rows(0, (x + 2) % NX)

    z_start(0)
    ring_start(1)
    ring_start(2)

    def halves(c):
        for r in range(0, 256, 32):
            high, low = split(blocks[c, r:r + 32, :])
            b_high[c, r:r + 32, :] = high
            b_low[c, r:r + 32, :] = low

    def owner_of(i, way):
        if i == 7:
            py, half = y, way
        else:
            step = i // 2 + 1
            py = (y + NY - step) % NY if way == 0 else (y + step) % NY
            half = half_of(way, i)
        return py // 2, 4 * (py % 2) + 2 * core + half

    def product(i):
        a = slab[i].reshape(32, DEPTH)
        f = dot_split(
            a, b_high[...].reshape(512, DEPTH), b_low[...].reshape(512, DEPTH), 1
        )
        for way in range(2):
            owner_x, owner_z = owner_of(i, way)
            slot = x_slots.at[owner_z, (x - owner_x + NX) % NX]
            for c in range(2):
                index = 4 * i + 2 * way + c
                r = 16 * way + 8 * c
                f_send[index] = f[r:r + 8, :]
                mine = jnp.logical_and(owner_x == x, core == c)

                @pl.when(mine)
                def _():
                    copy(f_send.at[index], slot, f_recv.at[owner_z]).start()

                @pl.when(jnp.logical_not(mine))
                def _():
                    remote(
                        f_send.at[index], slot, f_sem, f_recv.at[owner_z],
                        at(owner_x, z, y, c),
                    ).start()

    def apart(a):
        return jnp.minimum((a - y + NY) % NY, (y - a + NY) % NY)

    far = jnp.where(apart(2 * x) > apart(2 * x + 1), 0, 1)

    def over_z(which):
        arrived(x_slots.at[which], f_recv.at[which])
        total = x_slots[which, 0]
        for d in range(1, NX):
            total = total + x_slots[which, d]

        @pl.when(which == z)
        def _():
            z_slots[0] = total

        @pl.when(which != z)
        def _():
            q_send[which] = total
            remote(
                q_send.at[which], z_slots.at[(z - which + NZ) % NZ], q_sem, q_recv,
                at(x, which, y, core),
            ).start()

    for i in range(7):
        for sub in range(2):
            j = 2 * i + sub
            for way in range(2):
                ring[way, j].wait_recv()
                if j + 4 < 14:
                    ring[way, j + 4].start()
            if j == 0:
                for load in loads[3:]:
                    load.wait()
                halves(core)
            if j == 1:
                for hand in hands[:2]:
                    hand.wait_recv()
                halves(other)
            if j == 2:
                product(7)
            if j == 3:
                product(0)
            if sub == 0 and i >= 2:
                product(i - 1)
        for k in range(1, 3):
            if i in RING_AT[k - 1]:
                ring_step(k, RING_AT[k - 1].index(i))
        if i == X_AT:
            z_end(0)
            x_start(0)
    product(6)
    x_forward(0)
    for d in (0, 1, 3):
        one_to_mate(d, 4)
    for hand in hands[2:]:
        hand.wait_recv()
    for t in range(4):
        over_z(4 * (1 - far) + t)
    for t in range(4):
        over_z(4 * far + t)
    ring_step(1, 3)
    ring_step(2, 3)
    one_near()
    one_far()

    arrived(z_slots.at[pl.ds(1, NZ - 1)], q_recv)
    total = z_slots[0]
    for d in range(1, NZ):
        total = total + z_slots[d]
    residual = (
        jnp.concatenate([rhs[0, 0], rhs[0, 1], rhs[1, 0], rhs[1, 1]], axis=1) - total
    )

    def weights(ref, k):
        return ref[k].reshape(2048, 256)

    def of_block(b):
        return jnp.concatenate(
            [residual[:, 128 * b:128 * b + 128], residual[:, 256 + 128 * b:384 + 128 * b]], axis=1
        )

    terms = dot_split(of_block(0), weights(m_high, 0), weights(m_low, 0), 1)
    for k in range(NY):
        t_send[k] = terms[:, 256 * k:256 * k + 256]
    for d in (4, 3, 5, 2, 6, 1, 7):
        to = (y + d) % NY
        remote(
            t_send.at[to], t_slots.at[NY - 1 - d], stage_send.at[0], stage_recv.at[0],
            at(x, z, to, core),
        ).start()

    for k in range(1, 3):
        ring_step(k, 4)
        to_mate(k)
    second = of_block(1)
    arrived(t_slots, stage_recv.at[0])
    total = t_send[y]
    for d in range(NY - 1):
        total = total + t_slots[d]
    s_own[...] = total
    s_full[y] = total
    for d in (4, 3, 5, 2, 6, 1, 7):
        remote(
            s_own, s_full.at[y], stage_send.at[1], stage_recv.at[1],
            at(x, z, (y + d) % NY, core),
        ).start()
    s_mate[0] = total[:, :128]
    s_mate[1] = total[:, 128:]
    swap = remote(
        s_mate.at[other], s_mate.at[2], mate_send.at[7], mate_recv.at[7], mate
    )
    swap.start()
    panel(1)
    swap.wait()
    out[0, pl.ds(pl.multiple_of(8 * core, 8), 8), :] = s_mate[core]
    out[0, pl.ds(pl.multiple_of(8 * other, 8), 8), :] = s_mate[2]

    arrived(slab.at[pl.ds(0, 7)], y_send)
    for hand in hands:
        hand.wait_send()
    arrived(mats.at[core, 0, 0, pl.ds(0, 7)], zd_send)
    arrived(mats.at[core, pl.ds(1, 2), pl.ds(0, 3), 0], xd_send)
    arrived(mats.at[core, pl.ds(1, 2), pl.ds(0, 4), pl.ds(0, 7)], zr_send)
    for way in range(2):
        arrived(mats.at[core, 0, x], xr_send.at[0, way, 0])
        arrived(mats.at[core, 0, x, pl.ds(0, 4)], xr_send.at[0, way, 1])
    arrived(mats.at[core, 0, pl.ds(0, 3)], mate_send.at[4])
    arrived(mats.at[core, 0, 0], mate_send.at[8])
    for k in range(1, 3):
        arrived(mats.at[core, k], mate_send.at[4 + k])
    arrived(f_send.at[pl.ds(0, 28)], f_sem)
    arrived(q_send.at[pl.ds(0, 7)], q_sem)
    arrived(t_slots, stage_send.at[0])
    panel(2)

    arrived(s_full.at[pl.ds(0, 7)], stage_recv.at[1])
    solved = jnp.concatenate([s_full[k] for k in range(NY)], axis=1)
    second = second - dot_split(solved, weights(m_high, 1), weights(m_low, 1), 0)

    terms = dot_split(second, weights(m_high, 2), weights(m_low, 2), 1)
    for k in range(16):
        u_send[k] = terms[:, 128 * k:128 * k + 128]
    u_slots[8 * core + y] = u_send[col]
    for d in (8, 9, 7, 6, 10, 5, 11, 4, 12, 3, 13, 2, 14, 1, 15):
        to = (col + d) % 16
        remote(
            u_send.at[to], u_slots.at[8 * core + y], stage_send.at[2], stage_recv.at[2],
            (row, to),
        ).start()
    arrived(s_full.at[pl.ds(0, 7)], stage_send.at[1])
    arrived(u_slots.at[pl.ds(0, 15)], stage_recv.at[2])
    for half in range(2):
        total = u_slots[8 * half]
        for d in range(1, NY):
            total = total + u_slots[8 * half + d]
        out[1, 8 * half:8 * half + 8, :] = total
    arrived(u_slots.at[pl.ds(0, 15)], stage_send.at[2])


def per_device(
    prior_solved, block_one, block_two, cross_block, inverse_one, inverse_two, rhs_one, rhs_two
):
    vmem = pltpu.VMEM
    dma = pltpu.SemaphoreType.DMA
    out = pl.pallas_call(
        kernel,
        out_shape=jax.ShapeDtypeStruct((2, 16, 128), F32),
        in_specs=[pl.BlockSpec(memory_space=pltpu.HBM)] * 8,
        out_specs=pl.BlockSpec(memory_space=pltpu.VMEM),
        scratch_shapes=[
            vmem((8, 2, 16, DEPTH), F32),
            vmem((2, 256, DEPTH), F32),
            vmem((2, 256, DEPTH), BF16),
            vmem((2, 256, DEPTH), BF16),
            vmem((2, 3, NX, NZ, 64, 128), F32),
            vmem((3, NX, 512, 256), BF16),
            vmem((3, NX, 512, 256), BF16),
            vmem((2, 2, 8, 128), F32),
            vmem((32, 8, 512), F32),
            vmem((NZ, NX, 8, 512), F32),
            vmem((NZ, 8, 512), F32),
            vmem((NZ, 8, 512), F32),
            vmem((NY, 8, 256), F32),
            vmem((NY - 1, 8, 256), F32),
            vmem((8, 256), F32),
            vmem((NY, 8, 256), F32),
            vmem((3, 8, 128), F32),
            vmem((16, 8, 128), F32),
            vmem((16, 8, 128), F32),
            dma((9,)),
            dma,
            dma((2, 14)),
            dma((9,)),
            dma((9,)),
            dma,
            dma((1,)),
            dma,
            dma((2,)),
            dma,
            dma((2, 2, 4)),
            dma((1, 2, 2)),
            dma((1, 2, 2)),
            dma,
            dma((NZ,)),
            dma,
            dma,
            dma((3,)),
            dma((3,)),
        ],
        compiler_params=pltpu.CompilerParams(
            collective_id=0, has_side_effects=True, vmem_limit_bytes=62 * 1024 * 1024
        ),
    )(
        prior_solved.T, block_one, block_two, cross_block.T, inverse_one, inverse_two,
        rhs_one.T, rhs_two.T,
    )
    return out[0].T, out[1].T


def solution(mesh):
    placed = (
        P("row", "col"),
        P("col", "row"),
        P("col", "row"),
        P("col", "row"),
        P("row", "col"),
        P("row", "col"),
        P("col", "row"),
        P("col", "row"),
    )
    return jax.shard_map(
        per_device,
        mesh=mesh,
        in_specs=placed,
        out_specs=(P("col", "row"), P("col", "row")),
        check_vma=False,
    )
```
